32 devices in a mesh: gx: 4 (over z), gy: 4 (over y, x), gz: 2 (over core).
Axes of the slice: x: 2, y: 2, z: 4, core: 2. Of those that a mesh axis runs over, the one named last changes fastest.
Arguments:
- mass_per_volume: float32 [16, 64, 512], P('gz', 'gx', 'gy'), may hold values from 0.5 to 2
- flow_speed: float32 [3, 16, 64, 512], P(None, 'gz', 'gx', 'gy'), may hold values from -3 to 3
- pressure: float32 [16, 64, 512], P('gz', 'gx', 'gy'), may hold values from 0.5 to 2
- cotangent: float32 [5, 16, 64, 512], P(None, 'gz', 'gx', 'gy'), may hold values from -6 to 6
- weight_inner: float32 [64, 9], replicated, may hold values from -2 to 2
- weight_middle: float32 [64, 64], replicated, may hold values from -0.75 to 0.75
- weight_outer: float32 [64], replicated, may hold values from -0.75 to 0.75
Outputs:
- state_next: float32 [5, 16, 64, 512], P(None, 'gz', 'gx', 'gy')
- adjoint_density: float32 [16, 64, 512], P('gz', 'gx', 'gy')
- adjoint_velocity: float32 [3, 16, 64, 512], P(None, 'gz', 'gx', 'gy')
- adjoint_pressure: float32 [16, 64, 512], P('gz', 'gx', 'gy')
- adjoint_inner: float32 [64, 9], replicated
- adjoint_middle: float32 [64, 64], replicated
- adjoint_outer: float32 [64], replicated
The draws below stay inside these ranges and needn't reach their ends.
All inputs are finite; a program needn't handle non-finite values.
Results may differ from the reference program's by a relative error of at most 0.0003.
Values sent between devices are 32-bit elements; how exact they have to be, the bound alone decides.
A program may use at most 64 MiB of HBM per device.

```python
import math
import jax
import jax.numpy as jnp
from jax import lax

HID = 64
NX = 64
NY = 512
NZ = 16


def block_levels(own_key, dims, pieces, smallest, high):
    factor_of = 1.0
    for dim, blocks in pieces:
        heights = jax.random.uniform(jax.random.fold_in(jax.random.fold_in(own_key, 6), dim), (blocks,), jnp.float32, smallest / len(pieces), high / len(pieces))
        factor_of = factor_of * jnp.repeat(jnp.exp(heights), dims[dim] // blocks).reshape((-1,) + (1,) * (len(dims) - 1 - dim))
    return factor_of


def gaussian(own_key, dims, width, limit, pieces=(), kind=jnp.bfloat16):
    array = width * jax.random.normal(own_key, dims, jnp.float32)
    if pieces:
        array = array * block_levels(own_key, dims, pieces, -0.22, 0.18)
    return jnp.clip(array, -limit, limit).astype(kind)


def setup_inputs(seed: int = 0) -> dict:
    keys = jax.random.split(jax.random.key(seed), 8)
    return {
        "mass_per_volume": jnp.clip(0.5 + 1.5 * jax.random.uniform(keys[0], (NZ, NX, NY), jnp.float32) ** block_levels(keys[0], (NZ, NX, NY), ((0, 2), (1, 4), (2, 4)), -0.2, 0.2), 0.5, 2.0),
        "flow_speed": gaussian(keys[1], (3, NZ, NX, NY), 0.5, 3.0, ((1, 2), (2, 4), (3, 4)), jnp.float32),
        "pressure": jnp.clip(0.5 + 1.5 * jax.random.uniform(keys[2], (NZ, NX, NY), jnp.float32) ** block_levels(keys[2], (NZ, NX, NY), ((0, 2), (1, 4), (2, 4)), -0.2, 0.2), 0.5, 2.0),
        "cotangent": gaussian(keys[3], (5, NZ, NX, NY), 1.0, 6.0, ((1, 2), (2, 4), (3, 4)), jnp.float32),
        "weight_inner": gaussian(keys[4], (HID, 9), 9 ** -0.5, 2.0, (), jnp.float32),
        "weight_middle": gaussian(keys[5], (HID, HID), HID ** -0.5, 0.75, (), jnp.float32),
        "weight_outer": gaussian(keys[6], (HID,), HID ** -0.5, 0.75, (), jnp.float32),
    }


HEAT_RATIO = 1.4
THERMAL_DIFFUSE = 3.5
EDDY_SCALE = 0.5
TIME_STEP = 0.1
COMPACT_ALPHA = 1.0 / 3.0
COMPACT_NEAR = 14.0 / 9.0
COMPACT_FAR = 1.0 / 9.0
HIGHEST_PRECISION = lax.Precision.HIGHEST

def prepare(mass_per_volume, flow_speed, pressure):
    energy = pressure / (HEAT_RATIO - 1.0) + 0.5 * mass_per_volume * lax.optimization_barrier(jnp.sum(flow_speed * flow_speed, 0))
    state_now = jnp.concatenate([mass_per_volume[None], mass_per_volume[None] * flow_speed, energy[None]], 0)
    scalars = jnp.concatenate([flow_speed, (pressure / mass_per_volume)[None]], 0)
    return (state_now, scalars)

def fluxes(mass_per_volume, flow_speed, pressure, upstream_cotangent, eddy_viscosity):
    energy = pressure / (HEAT_RATIO - 1.0) + 0.5 * mass_per_volume * lax.optimization_barrier(jnp.sum(flow_speed * flow_speed, 0))
    attenuation_coefficient = mass_per_volume * eddy_viscosity
    stagnation_specific_energy = energy + pressure
    directions = []
    for traversal_axis in range(3):
        transported_array = flow_speed[traversal_axis]
        partition_parts = [mass_per_volume * transported_array]
        for coordinate_slot in range(3):
            mass_flux_array = mass_per_volume * flow_speed[coordinate_slot] * transported_array - attenuation_coefficient * upstream_cotangent[traversal_axis, coordinate_slot]
            if coordinate_slot == traversal_axis:
                mass_flux_array = mass_flux_array + pressure
            partition_parts.append(mass_flux_array)
        partition_parts.append(stagnation_specific_energy * transported_array - THERMAL_DIFFUSE * attenuation_coefficient * upstream_cotangent[traversal_axis, 3])
        directions.append(jnp.stack(partition_parts))
    return jnp.stack(directions)

def derive_x(values):
    spectrum = jnp.fft.rfft(values, axis=-2)
    wavenumber = 2.0 * math.pi * jnp.arange(NX // 2 + 1, dtype=jnp.float32) / NX
    symbol = (COMPACT_NEAR * jnp.sin(wavenumber) + 0.5 * COMPACT_FAR * jnp.sin(2.0 * wavenumber)) / (1.0 + 2.0 * COMPACT_ALPHA * jnp.cos(wavenumber))
    return jnp.fft.irfft(spectrum * (1j * symbol)[:, None], n=NX, axis=-2)

def explicit(values, along_axis):

    def shifted(offset):
        return jnp.roll(values, -offset, axis=along_axis)
    return (45.0 * (shifted(1) - shifted(-1)) - 9.0 * (shifted(2) - shifted(-2)) + (shifted(3) - shifted(-3))) / 60.0

def viscosity(upstream_cotangent, inner_weight, middle_weight, outer_weight):
    features = upstream_cotangent[:, :3].reshape((9,) + upstream_cotangent.shape[2:])
    planes = jnp.moveaxis(features, 1, 0)

    def one_plane(plane_features):
        hidden = jnp.tanh(jnp.einsum('hc,cxy->hxy', inner_weight, plane_features, precision=HIGHEST_PRECISION))
        hidden = jnp.tanh(jnp.einsum('hk,kxy->hxy', middle_weight, hidden, precision=HIGHEST_PRECISION))
        output = jnp.einsum('h,hxy->xy', outer_weight, hidden, precision=HIGHEST_PRECISION)
        return EDDY_SCALE * jax.nn.softplus(output)
    return lax.map(jax.checkpoint(one_plane), planes)

def forward(mass_per_volume, flow_speed, pressure, weight_inner, weight_middle, weight_outer):
    state_now, scalars = prepare(mass_per_volume, flow_speed, pressure)
    gradients = jnp.stack([derive_x(scalars), explicit(scalars, -1), explicit(scalars, -3)])
    eddy_viscosity = viscosity(gradients, weight_inner, weight_middle, weight_outer)
    flux_all = fluxes(mass_per_volume, flow_speed, pressure, gradients, eddy_viscosity)
    divergence = derive_x(flux_all[0]) + explicit(flux_all[1], -1) + explicit(flux_all[2], -3)
    return state_now - TIME_STEP * divergence

def reference(mass_per_volume, flow_speed, pressure, cotangent, weight_inner, weight_middle, weight_outer):
    state_next, pullback = jax.vjp(forward, mass_per_volume, flow_speed, pressure, weight_inner, weight_middle, weight_outer)
    pulled = pullback(cotangent)
    factor = 1.0 / math.sqrt(NX * NY * NZ)
    return (state_next, pulled[0], pulled[1], pulled[2], pulled[3] * factor, pulled[4] * factor, pulled[5] * factor)
```

```python
import functools
import math

import jax
import jax.numpy as jnp
import ml_dtypes
import numpy as np
from jax import lax
from jax.experimental import pallas as pl
from jax.experimental.pallas import tpu as pltpu
from jax.sharding import PartitionSpec as P

TIME_STEP = 0.1
ALPHA = 1.0 / 3.0
MESH = pl.DeviceIdType.MESH
F32 = jnp.float32
BF16 = jnp.bfloat16
ROOT = (-1.0 + math.sqrt(1.0 - 4.0 * ALPHA**2)) / (2.0 * ALPHA)
FIELDS = 9
HID = 64


def split_np(a):
    hi = a.astype(ml_dtypes.bfloat16)
    lo = (a - hi.astype(np.float64)).astype(ml_dtypes.bfloat16)
    return np.concatenate([hi, lo, hi], 1)


def split(x):
    hi = x.astype(BF16)
    lo = (x - hi.astype(F32)).astype(BF16)
    return hi, lo


def stack3(x):
    hi, lo = split(x)
    return jnp.concatenate([hi, hi, lo], 0)


def x_tables(xc, zc, groups):
    n = xc * groups
    r = ROOT
    c0 = 1.0 + 2.0 * ALPHA * r
    period = 1.0 - r**n
    gain = (7.0 / 9.0 * (r - 1 / r) + 1.0 / 36.0 * (r**2 - r**-2)) / c0
    fix = (1 / r - r) / 36.0 / c0
    i = np.arange(xc)
    d = i[:, None] - i[None, :]
    own = np.where(d == 0, 0.0, np.sign(d) * gain * r ** np.abs(d))
    own = own + np.where(np.abs(d) == 1, np.sign(d) * fix, 0.0)
    own = own + gain * (r ** (d + n) - r ** (n - d)) / period
    eye = np.eye(zc)
    last = np.zeros((1, xc))
    last[0, -1] = 1.0
    first = np.zeros((1, xc))
    first[0, 0] = 1.0
    right = (r ** (xc - 1 - i))[None]
    left = (r**i)[None]
    full = np.concatenate(
        [np.kron(eye, own)] + [np.kron(eye, row) for row in (last, right, left, first)], 0
    )
    add_last = np.zeros((xc, 1))
    add_last[0] = fix
    add_first = np.zeros((xc, 1))
    add_first[-1] = -fix
    add = np.concatenate(
        [
            np.kron(eye, column)
            for column in (
                add_last,
                (gain * r ** (i + 1))[:, None],
                (-gain * r ** (xc - i))[:, None],
                add_first,
            )
        ],
        1,
    )
    return split_np(full), split_np(add)


def kernel(
    dims, offsets, rho_ref, vel_ref, prs_ref, ct_ref, xfull_ref, xadd_ref, w1_ref, w2_ref, w2t_ref,
    b1_ref, w3_ref, next_ref, arho_ref, avel_ref, aprs_ref, wg_ref,
    f0, fx, fy, fz, der, back, w1s, w2s, w2ts, b1s, acc, w3acc,
    mom, momr, ypl, ypr, yl, yr, zlo, zhi, part_z, part_x, part_y, send_sem, recv_sem,
):
    gxn, gyn, gzn = dims
    sizes = {"gx": gxn, "gy": gyn, "gz": gzn}
    me = {axis: lax.axis_index(axis) for axis in sizes}
    lane = lax.broadcasted_iota(jnp.int32, (1, 1, 128), 2)

    def other(axis, offset):
        return {axis: lax.rem(me[axis] + (offset + sizes[axis]), sizes[axis])}

    barrier = pltpu.get_barrier_semaphore()
    total = 0
    for axis in sizes:
        for offset in range(1, sizes[axis]):
            pl.semaphore_signal(barrier, inc=1, device_id=other(axis, offset), device_id_type=MESH)
            total += 1

    used = [0]

    def remote(src, dst, axis, offset):
        k = used[0]
        used[0] += 1
        copy = pltpu.make_async_remote_copy(
            src_ref=src, dst_ref=dst, send_sem=send_sem.at[k], recv_sem=recv_sem.at[k],
            device_id=other(axis, offset), device_id_type=MESH,
        )
        copy.start()
        return copy

    pending = []

    def send_z(ph, src):
        a = remote(src.at[:, 10:16], zlo.at[ph], "gz", 1)
        b = remote(src.at[:, 0:6], zhi.at[ph], "gz", -1)
        return [a, b]

    def send_y(ph, src):
        for j in range(FIELDS):
            for q in range(4):
                block = src[j, 4 * q : 4 * q + 4]
                at = 32 * q + 3 * j
                inside = (lane >= at) & (lane < at + 3)
                hi_edge = pltpu.roll(block, (at - 125) % 128, 2)
                lo_edge = pltpu.roll(block, at, 2) if at else block
                if j == 0 and q == 0:
                    vl, vr = hi_edge, lo_edge
                    keep = [vl, vr]
                else:
                    keep = [
                        jnp.where(inside, hi_edge, keep[0]),
                        jnp.where(inside, lo_edge, keep[1]),
                    ]
        ypl[ph] = keep[0]
        ypr[ph] = keep[1]
        return [
            remote(ypl.at[ph], yl.at[ph], "gy", 1),
            remote(ypr.at[ph], yr.at[ph], "gy", -1),
        ]

    def send_x(ph, src, put):
        def one(j, carry):
            y = jnp.dot(
                xfull_ref[...], stack3(src[j].reshape(128, 128)), preferred_element_type=F32
            )
            put(j, y[:128].reshape(16, 8, 128))
            for m in range(4):
                mom[ph, m, j] = y[128 + 8 * m : 136 + 8 * m]
            return carry

        lax.fori_loop(0, FIELDS, one, 0, unroll=3)
        copies = []
        for slot, offset in enumerate(offsets):
            lo = 0 if offset == 1 else 1
            hi = 4 if offset == -1 else 3
            copies.append(
                remote(mom.at[ph, lo:hi], momr.at[ph, slot, lo:hi], "gx", offset)
            )
        return copies

    def dy(ph, src, j):
        outs = []
        for q in range(4):
            at = 32 * q + 3 * j
            f = src[j, 4 * q : 4 * q + 4]
            el = pltpu.roll(yl[ph], (125 - at) % 128, 2)
            er = pltpu.roll(yr[ph], (-at) % 128, 2) if at else yr[ph]

            def ahead(s):
                return pltpu.roll(jnp.where(lane < s, er, f), 128 - s, 2)

            def behind(s):
                return pltpu.roll(jnp.where(lane >= 128 - s, el, f), s, 2)

            outs.append(
                0.75 * (ahead(1) - behind(1))
                - 0.15 * (ahead(2) - behind(2))
                + (1.0 / 60.0) * (ahead(3) - behind(3))
            )
        return jnp.concatenate(outs, 0)

    def dz(ph, src, j):
        ext = jnp.concatenate([zlo[ph, j], src[j], zhi[ph, j]], 0)

        def shifted(s):
            return ext[6 + 2 * s : 22 + 2 * s]

        return (
            0.75 * (shifted(1) - shifted(-1))
            - 0.15 * (shifted(2) - shifted(-2))
            + (1.0 / 60.0) * (shifted(3) - shifted(-3))
        )

    period = 1.0 - ROOT ** (16 * gxn)

    def add_x(ph, add):
        def one(j, carry):
            va = jnp.zeros((8, 128), F32)
            vb = jnp.zeros((8, 128), F32)
            for slot, offset in enumerate(offsets):
                wa = ROOT ** (16 * (offset % gxn - 1)) / period
                wb = ROOT ** (16 * ((-offset) % gxn - 1)) / period
                va = va + wa * momr[ph, slot, 1, j]
                vb = vb + wb * momr[ph, slot, 2, j]
            rows = jnp.concatenate(
                [
                    momr[ph, offsets.index(1), 0, j],
                    va,
                    vb,
                    momr[ph, offsets.index(-1), 3, j],
                ],
                0,
            )
            y = jnp.dot(xadd_ref[...], stack3(rows), preferred_element_type=F32)
            add(j, y.reshape(16, 8, 128))
            return carry

        lax.fori_loop(0, FIELDS, one, 0, unroll=3)

    f0[0:3] = vel_ref[...]
    f0[3] = prs_ref[...] / rho_ref[...]
    f0[4:9] = ct_ref[...]
    pl.semaphore_wait(barrier, total)
    cz = send_z(0, f0)
    cy = send_y(0, f0)

    def put0(j, value):
        der[0, j] = value

    cx = send_x(0, f0, put0)
    pending += cz + cy + cx

    def halves(src, dst, third):
        x = src[...]
        hi, lo = split(x)
        col = lax.broadcasted_iota(jnp.int32, x.shape, 1)
        mid = (col >= third) & (col < 2 * third)
        dst[...] = jnp.where(mid, lo.astype(F32), hi.astype(F32)).astype(BF16)

    halves(w1_ref, w1s, 80)
    halves(w2_ref, w2s, HID)
    halves(w2t_ref, w2ts, HID)
    halves(b1_ref, b1s, 8 * HID)
    acc[...] = jnp.zeros_like(acc)
    w3acc[...] = jnp.zeros_like(w3acc)

    for c in cz:
        c.wait_recv()
    for j in range(FIELDS):
        der[2, j] = dz(0, f0, j)
    for c in cy:
        c.wait_recv()
    for j in range(FIELDS):
        der[1, j] = dy(0, f0, j)
    for c in cx:
        c.wait_recv()

    def add0(j, value):
        der[0, j] = der[0, j] + value

    add_x(0, add0)

    sub = lax.broadcasted_iota(jnp.int32, (8, 128), 0)

    def group(g, carry):
        feats = [der[k, i, g] for k in range(3) for i in range(3)]
        pre = jnp.dot(
            w1s[...],
            stack3(jnp.concatenate(feats + [jnp.zeros((8, 128), F32)], 0)),
            preferred_element_type=F32,
        )
        h1 = jnp.tanh(
            jnp.concatenate([pre[80 * x : 80 * x + 64] for x in range(8)], 1)
        )
        ft = jnp.concatenate([pre[80 * x + 64 : 80 * x + 80] for x in range(8)], 1)
        h1h, h1l = split(h1)
        h2 = jnp.tanh(
            jnp.dot(
                w2s[...], jnp.concatenate([h1h, h1h, h1l], 0), preferred_element_type=F32
            )
        )
        w3 = w3_ref[...]
        o = jnp.zeros((8, 128), F32)
        for x in range(8):
            row = jnp.sum(h2[:, 128 * x : 128 * x + 128] * w3, 0, keepdims=True)
            o = jnp.where(sub == x, row, o)
        decay = jnp.exp(-jnp.abs(o))
        eddy = 0.5 * (jnp.maximum(o, 0.0) + jnp.log1p(decay))
        sig = jnp.where(o >= 0.0, 1.0, decay) / (1.0 + decay)

        rho = rho_ref[g]
        prs = prs_ref[g]
        u = [vel_ref[i, g] for i in range(3)]
        ct = [ct_ref[i, g] for i in range(5)]
        q = u[0] * u[0] + u[1] * u[1] + u[2] * u[2]
        energy = prs / 0.4 + 0.5 * rho * q
        stag = energy + prs
        att = rho * eddy
        s = [[TIME_STEP * der[k, 4 + m, g] for m in range(5)] for k in range(3)]
        grad3 = [der[k, 3, g] for k in range(3)]
        flux_refs = (fx, fy, fz)
        att_bar = jnp.zeros((8, 128), F32)
        rho_bar = jnp.zeros((8, 128), F32)
        stag_bar = s[0][4] * u[0] + s[1][4] * u[1] + s[2][4] * u[2]
        for k in range(3):
            ref = flux_refs[k]
            mass = rho * u[k]
            ref[4, g] = mass
            inner = s[k][0]
            for i in range(3):
                value = mass * u[i] - att * feats[3 * k + i]
                if i == k:
                    value = value + prs
                ref[5 + i, g] = value
                att_bar = att_bar - s[k][1 + i] * feats[3 * k + i]
                inner = inner + s[k][1 + i] * u[i]
            ref[8, g] = stag * u[k] - 3.5 * att * grad3[k]
            ref[3, g] = -3.5 * att * s[k][4]
            att_bar = att_bar - 3.5 * s[k][4] * grad3[k]
            rho_bar = rho_bar + inner * u[k]
        for j in range(3):
            t = s[j][0] + ct[1 + j] + (stag_bar + ct[4]) * u[j]
            for i in range(3):
                t = t + (s[j][1 + i] + s[i][1 + j]) * u[i]
            avel_ref[j, g] = rho * t + stag * s[j][4]
        aprs_ref[g] = s[0][1] + s[1][2] + s[2][3] + stag_bar + (stag_bar + ct[4]) / 0.4
        arho_ref[g] = (
            rho_bar + 0.5 * q * (stag_bar + ct[4]) + att_bar * eddy + ct[0]
            + ct[1] * u[0] + ct[2] * u[1] + ct[3] * u[2]
        )
        next_ref[0, g] = rho
        for i in range(3):
            next_ref[1 + i, g] = rho * u[i]
        next_ref[4, g] = energy

        ob = 0.5 * att_bar * rho * sig
        seeds = []
        outer = w3acc[...]
        for x in range(8):
            row = jnp.broadcast_to(ob[x : x + 1], (HID, 128))
            seeds.append(row * w3)
            outer = outer + row * h2[:, 128 * x : 128 * x + 128]
        w3acc[...] = outer
        a2 = jnp.concatenate(seeds, 1) * (1.0 - h2 * h2)
        a2h, a2l = split(a2)
        a1 = jnp.dot(
            w2ts[...], jnp.concatenate([a2h, a2h, a2l], 0), preferred_element_type=F32
        ) * (1.0 - h1 * h1)
        a1h, a1l = split(a1)
        tall_h = jnp.concatenate([a1h[:, 128 * x : 128 * x + 128] for x in range(8)], 0)
        tall_l = jnp.concatenate([a1l[:, 128 * x : 128 * x + 128] for x in range(8)], 0)
        fbar = jnp.dot(
            b1s[...], jnp.concatenate([tall_h, tall_h, tall_l], 0), preferred_element_type=F32
        )
        for k in range(3):
            for i in range(3):
                c = 3 * k + i
                flux_refs[k][i, g] = fbar[8 * c : 8 * c + 8] - att * s[k][1 + i]
        fth, ftl = split(ft)
        acc[:, :160] = acc[:, :160] + lax.dot_general(
            jnp.concatenate([a2h, a2l, a1h, a1l], 0),
            jnp.concatenate([h1h, h1l, fth, ftl], 0),
            (((1,), (1,)), ((), ())),
            preferred_element_type=F32,
        )
        return carry

    lax.fori_loop(0, 16, group, 0)

    wlane = lax.broadcasted_iota(jnp.int32, (HID, 128), 1)
    mid_w = acc[0:64, 0:128] + acc[64:128, 0:128] + pltpu.roll(acc[0:64, 0:128], 64, 1)
    in_w = acc[128:192, 128:256] + acc[192:256, 128:256]
    in_w = in_w + pltpu.roll(acc[128:192, 128:256], 112, 1)
    in_w = pltpu.roll(in_w, 64, 1)
    out_w = jnp.sum(w3acc[...], 1, keepdims=True)
    mine = jnp.where(
        wlane < 64, mid_w, jnp.where(wlane < 80, in_w, jnp.where(wlane == 80, out_w, 0.0))
    )

    def exchange(buf, axis, value):
        buf[me[axis]] = value
        return [
            remote(buf.at[me[axis]], buf.at[me[axis]], axis, offset)
            for offset in range(1, sizes[axis])
        ]

    def total_of(buf, axis):
        value = buf[0]
        for i in range(1, sizes[axis]):
            value = value + buf[i]
        return value

    ez = exchange(part_z, "gz", mine)
    cz = send_z(1, fz)
    cy = send_y(1, fy)

    def put1(j, value):
        back[j] = value

    cx = send_x(1, fx, put1)
    for c in ez:
        c.wait_recv()
    ex = exchange(part_x, "gx", total_of(part_z, "gz"))
    for c in cz:
        c.wait_recv()
    for j in range(FIELDS):
        back[j] = back[j] + dz(1, fz, j)
    for c in cy:
        c.wait_recv()
    for j in range(FIELDS):
        back[j] = back[j] + dy(1, fy, j)
    for c in ex:
        c.wait_recv()
    ey = exchange(part_y, "gy", total_of(part_x, "gx"))
    for c in cx:
        c.wait_recv()

    def add1(j, value):
        back[j] = back[j] + value

    add_x(1, add1)
    for m in range(5):
        next_ref[m] = next_ref[m] - TIME_STEP * back[4 + m]
    for j in range(3):
        avel_ref[j] = avel_ref[j] - back[j]
    inv = 1.0 / rho_ref[...]
    heat = back[3] * inv
    aprs_ref[...] = aprs_ref[...] - heat
    arho_ref[...] = arho_ref[...] + heat * f0[3]
    for c in ey:
        c.wait_recv()
    cells = 16384 * gxn * gyn * gzn
    wg_ref[...] = total_of(part_y, "gy") * (1.0 / math.sqrt(cells))
    pending += ez + cz + cy + cx + ex + ey
    for c in pending:
        c.wait_send()


def local(dims, rho, vel, prs, ct, w_in, w_mid, w_out):
    gxn, gyn, gzn = dims
    zc, xc, yc = rho.shape
    reach = 40 // xc + 2
    if 2 * reach + 1 >= gxn:
        offsets = list(range(1, gxn - 1)) + [-1]
    else:
        offsets = list(range(1, reach + 1)) + list(range(-reach, 0))
    offsets = tuple(offsets)
    n_off = len(offsets)
    xfull, xadd = x_tables(xc, zc, gxn)
    feat = jnp.concatenate(
        [jnp.pad(w_in, ((0, 0), (0, 1))), jnp.asarray(np.eye(16, 10), F32)], 0
    )
    eye = jnp.asarray(np.eye(8), F32)
    w1 = (eye[:, None, None, :] * feat[None, :, :, None]).reshape(640, 80)
    w1 = jnp.concatenate([w1, w1, w1], 1)
    b1 = jnp.pad(w_in, ((0, 0), (0, 1))).T[:, None, None, :] * eye[None, :, :, None]
    b1 = b1.reshape(80, 512)
    b1 = jnp.concatenate([b1, b1, b1], 1)
    w2 = jnp.concatenate([w_mid, w_mid, w_mid], 1)
    w2t = jnp.concatenate([w_mid.T, w_mid.T, w_mid.T], 1)
    w3 = jnp.broadcast_to(w_out[:, None], (HID, 128))
    block = (16, 8, 128)
    n_sem = 2 * (n_off + 4) + (gxn - 1) + (gyn - 1) + (gzn - 1)
    vmem = pl.BlockSpec(memory_space=pltpu.VMEM)
    out = pl.pallas_call(
        functools.partial(kernel, dims, offsets),
        out_shape=(
            jax.ShapeDtypeStruct((5,) + block, F32),
            jax.ShapeDtypeStruct(block, F32),
            jax.ShapeDtypeStruct((3,) + block, F32),
            jax.ShapeDtypeStruct(block, F32),
            jax.ShapeDtypeStruct((HID, 128), F32),
        ),
        in_specs=[vmem] * 11,
        out_specs=(vmem,) * 5,
        scratch_shapes=[
            pltpu.VMEM((FIELDS,) + block, F32),
            pltpu.VMEM((FIELDS,) + block, F32),
            pltpu.VMEM((FIELDS,) + block, F32),
            pltpu.VMEM((FIELDS,) + block, F32),
            pltpu.VMEM((3, FIELDS) + block, F32),
            pltpu.VMEM((FIELDS,) + block, F32),
            pltpu.VMEM((640, 240), BF16),
            pltpu.VMEM((HID, 192), BF16),
            pltpu.VMEM((HID, 192), BF16),
            pltpu.VMEM((80, 1536), BF16),
            pltpu.VMEM((256, 256), F32),
            pltpu.VMEM((HID, 128), F32),
            pltpu.VMEM((2, 4, FIELDS, 8, 128), F32),
            pltpu.VMEM((2, n_off, 4, FIELDS, 8, 128), F32),
            pltpu.VMEM((2, 4, 8, 128), F32),
            pltpu.VMEM((2, 4, 8, 128), F32),
            pltpu.VMEM((2, 4, 8, 128), F32),
            pltpu.VMEM((2, 4, 8, 128), F32),
            pltpu.VMEM((2, FIELDS, 6, 8, 128), F32),
            pltpu.VMEM((2, FIELDS, 6, 8, 128), F32),
            pltpu.VMEM((gzn, HID, 128), F32),
            pltpu.VMEM((gxn, HID, 128), F32),
            pltpu.VMEM((gyn, HID, 128), F32),
            pltpu.SemaphoreType.DMA((n_sem,)),
            pltpu.SemaphoreType.DMA((n_sem,)),
        ],
        compiler_params=pltpu.CompilerParams(
            collective_id=0, has_side_effects=True, vmem_limit_bytes=40 * 1024 * 1024
        ),
    )(
        rho.reshape(block), vel.reshape((3,) + block), prs.reshape(block), ct.reshape((5,) + block),
        jnp.asarray(xfull), jnp.asarray(xadd), w1, w2, w2t, b1, w3,
    )
    nxt, arho, avel, aprs, wg = out
    return (
        nxt.reshape(ct.shape),
        arho.reshape(rho.shape),
        avel.reshape(vel.shape),
        aprs.reshape(prs.shape),
        wg[:, 64:73],
        wg[:, :64],
        wg[:, 80],
    )


def solution(mesh):
    dims = tuple(mesh.shape[axis] for axis in ("gx", "gy", "gz"))
    placed = (
        P("gz", "gx", "gy"),
        P(None, "gz", "gx", "gy"),
        P("gz", "gx", "gy"),
        P(None, "gz", "gx", "gy"),
        P(),
        P(),
        P(),
    )
    return jax.shard_map(
        functools.partial(local, dims),
        mesh=mesh,
        in_specs=placed,
        out_specs=(
            P(None, "gz", "gx", "gy"),
            P("gz", "gx", "gy"),
            P(None, "gz", "gx", "gy"),
            P("gz", "gx", "gy"),
            P(),
            P(),
            P(),
        ),
        check_vma=False,
    )
```

```python
import functools
import math

import jax
import jax.numpy as jnp
import ml_dtypes
import numpy as np
from jax import lax
from jax.experimental import pallas as pl
from jax.experimental.pallas import tpu as pltpu
from jax.sharding import PartitionSpec as P

TIME_STEP = 0.1
ALPHA = 1.0 / 3.0
MESH = pl.DeviceIdType.MESH
F32 = jnp.float32
BF16 = jnp.bfloat16
ROOT = (-1.0 + math.sqrt(1.0 - 4.0 * ALPHA**2)) / (2.0 * ALPHA)
FIELDS = 9
HID = 64


def split_np(a):
    hi = a.astype(ml_dtypes.bfloat16)
    lo = (a - hi.astype(np.float64)).astype(ml_dtypes.bfloat16)
    return np.concatenate([hi, lo, hi], 1)


def split(x):
    hi = x.astype(BF16)
    lo = (x - hi.astype(F32)).astype(BF16)
    return hi, lo


def stack3(x):
    hi, lo = split(x)
    return jnp.concatenate([hi, hi, lo], 0)


def x_tables(xc, zc, groups):
    n = xc * groups
    r = ROOT
    c0 = 1.0 + 2.0 * ALPHA * r
    period = 1.0 - r**n
    gain = (7.0 / 9.0 * (r - 1 / r) + 1.0 / 36.0 * (r**2 - r**-2)) / c0
    fix = (1 / r - r) / 36.0 / c0
    i = np.arange(xc)
    d = i[:, None] - i[None, :]
    own = np.where(d == 0, 0.0, np.sign(d) * gain * r ** np.abs(d))
    own = own + np.where(np.abs(d) == 1, np.sign(d) * fix, 0.0)
    own = own + gain * (r ** (d + n) - r ** (n - d)) / period
    eye = np.eye(zc)
    last = np.zeros((1, xc))
    last[0, -1] = 1.0
    first = np.zeros((1, xc))
    first[0, 0] = 1.0
    right = (r ** (xc - 1 - i))[None]
    left = (r**i)[None]
    full = np.concatenate(
        [np.kron(eye, own)] + [np.kron(eye, row) for row in (last, right, left, first)], 0
    )
    add_last = np.zeros((xc, 1))
    add_last[0] = fix
    add_first = np.zeros((xc, 1))
    add_first[-1] = -fix
    add = np.concatenate(
        [
            np.kron(eye, column)
            for column in (
                add_last,
                (gain * r ** (i + 1))[:, None],
                (-gain * r ** (xc - i))[:, None],
                add_first,
            )
        ],
        1,
    )
    return split_np(full), split_np(add)


def kernel(
    dims, offsets, rho_ref, vel_ref, prs_ref, ct_ref, xfull_ref, xadd_ref, w1_ref, w2_ref, w2t_ref,
    b1_ref, w3_ref, next_ref, arho_ref, avel_ref, aprs_ref, wg_ref,
    f0, fx, fy, fz, der, back, w1s, w2s, w2ts, b1s, acc, w3acc,
    mom, momr, ypl, ypr, yl, yr, zlo, zhi, part_z, part_x, part_y, send_sem, recv_sem,
):
    gxn, gyn, gzn = dims
    sizes = {"gx": gxn, "gy": gyn, "gz": gzn}
    me = {axis: lax.axis_index(axis) for axis in sizes}
    lane = lax.broadcasted_iota(jnp.int32, (1, 1, 128), 2)

    def other(axis, offset):
        return {axis: lax.rem(me[axis] + (offset + sizes[axis]), sizes[axis])}

    barrier = pltpu.get_barrier_semaphore()
    total = 0
    for axis in sizes:
        for offset in range(1, sizes[axis]):
            pl.semaphore_signal(barrier, inc=1, device_id=other(axis, offset), device_id_type=MESH)
            total += 1

    used = [0]

    def remote(src, dst, axis, offset):
        k = used[0]
        used[0] += 1
        copy = pltpu.make_async_remote_copy(
            src_ref=src, dst_ref=dst, send_sem=send_sem.at[k], recv_sem=recv_sem.at[k],
            device_id=other(axis, offset), device_id_type=MESH,
        )
        copy.start()
        return copy

    pending = []

    def send_z(ph, src):
        a = remote(src.at[:, 10:16], zlo.at[ph], "gz", 1)
        b = remote(src.at[:, 0:6], zhi.at[ph], "gz", -1)
        return [a, b]

    def pack_y(ph, src):
        for j in range(FIELDS):
            for q in range(4):
                block = src[j, 4 * q : 4 * q + 4]
                at = 32 * q + 3 * j
                inside = (lane >= at) & (lane < at + 3)
                hi_edge = pltpu.roll(block, (at - 125) % 128, 2)
                lo_edge = pltpu.roll(block, at, 2) if at else block
                if j == 0 and q == 0:
                    vl, vr = hi_edge, lo_edge
                    keep = [vl, vr]
                else:
                    keep = [
                        jnp.where(inside, hi_edge, keep[0]),
                        jnp.where(inside, lo_edge, keep[1]),
                    ]
        ypl[ph] = keep[0]
        ypr[ph] = keep[1]

    def start_y(ph):
        return [
            remote(ypl.at[ph], yl.at[ph], "gy", 1),
            remote(ypr.at[ph], yr.at[ph], "gy", -1),
        ]

    def solve_x(ph, src, put):
        def one(j, carry):
            y = jnp.dot(
                xfull_ref[...], stack3(src[j].reshape(128, 128)), preferred_element_type=F32
            )
            put(j, y[:128].reshape(16, 8, 128))
            for m in range(4):
                mom[ph, m, j] = y[128 + 8 * m : 136 + 8 * m]
            return carry

        lax.fori_loop(0, FIELDS, one, 0, unroll=9)

    def start_x(ph):
        copies = []
        for slot, offset in enumerate(offsets):
            lo = 0 if offset == 1 else 1
            hi = 4 if offset == -1 else 3
            copies.append(
                remote(mom.at[ph, lo:hi], momr.at[ph, slot, lo:hi], "gx", offset)
            )
        return copies

    def dy(ph, src, j):
        outs = []
        for q in range(4):
            at = 32 * q + 3 * j
            f = src[j, 4 * q : 4 * q + 4]
            el = pltpu.roll(yl[ph], (125 - at) % 128, 2)
            er = pltpu.roll(yr[ph], (-at) % 128, 2) if at else yr[ph]

            def ahead(s):
                return pltpu.roll(jnp.where(lane < s, er, f), 128 - s, 2)

            def behind(s):
                return pltpu.roll(jnp.where(lane >= 128 - s, el, f), s, 2)

            outs.append(
                0.75 * (ahead(1) - behind(1))
                - 0.15 * (ahead(2) - behind(2))
                + (1.0 / 60.0) * (ahead(3) - behind(3))
            )
        return jnp.concatenate(outs, 0)

    def dz(ph, src, j):
        ext = jnp.concatenate([zlo[ph, j], src[j], zhi[ph, j]], 0)

        def shifted(s):
            return ext[6 + 2 * s : 22 + 2 * s]

        return (
            0.75 * (shifted(1) - shifted(-1))
            - 0.15 * (shifted(2) - shifted(-2))
            + (1.0 / 60.0) * (shifted(3) - shifted(-3))
        )

    period = 1.0 - ROOT ** (16 * gxn)

    def add_x(ph, add):
        def one(j, carry):
            va = jnp.zeros((8, 128), F32)
            vb = jnp.zeros((8, 128), F32)
            for slot, offset in enumerate(offsets):
                wa = ROOT ** (16 * (offset % gxn - 1)) / period
                wb = ROOT ** (16 * ((-offset) % gxn - 1)) / period
                va = va + wa * momr[ph, slot, 1, j]
                vb = vb + wb * momr[ph, slot, 2, j]
            rows = jnp.concatenate(
                [
                    momr[ph, offsets.index(1), 0, j],
                    va,
                    vb,
                    momr[ph, offsets.index(-1), 3, j],
                ],
                0,
            )
            y = jnp.dot(xadd_ref[...], stack3(rows), preferred_element_type=F32)
            add(j, y.reshape(16, 8, 128))
            return carry

        lax.fori_loop(0, FIELDS, one, 0, unroll=9)

    f0[0:3] = vel_ref[...]
    f0[3] = prs_ref[...] / rho_ref[...]
    f0[4:9] = ct_ref[...]

    def put0(j, value):
        der[0, j] = value

    solve_x(0, f0, put0)
    pl.semaphore_wait(barrier, total)
    cx = start_x(0)
    cz = send_z(0, f0)
    pack_y(0, f0)
    cy = start_y(0)
    pending += cz + cy + cx

    def halves(src, dst, third):
        x = src[...]
        hi, lo = split(x)
        col = lax.broadcasted_iota(jnp.int32, x.shape, 1)
        mid = (col >= third) & (col < 2 * third)
        dst[...] = jnp.where(mid, lo.astype(F32), hi.astype(F32)).astype(BF16)

    halves(w1_ref, w1s, 80)
    halves(w2_ref, w2s, HID)
    halves(w2t_ref, w2ts, HID)
    halves(b1_ref, b1s, 8 * HID)
    acc[...] = jnp.zeros_like(acc)
    w3acc[...] = jnp.zeros_like(w3acc)

    for c in cz:
        c.wait_recv()
    for j in range(FIELDS):
        der[2, j] = dz(0, f0, j)
    for c in cy:
        c.wait_recv()
    for j in range(FIELDS):
        der[1, j] = dy(0, f0, j)
    for c in cx:
        c.wait_recv()

    def add0(j, value):
        der[0, j] = der[0, j] + value

    add_x(0, add0)

    sub = lax.broadcasted_iota(jnp.int32, (8, 128), 0)

    def group(g, carry):
        feats = [der[k, i, g] for k in range(3) for i in range(3)]
        pre = jnp.dot(
            w1s[...],
            stack3(jnp.concatenate(feats + [jnp.zeros((8, 128), F32)], 0)),
            preferred_element_type=F32,
        )
        h1 = jnp.tanh(
            jnp.concatenate([pre[80 * x : 80 * x + 64] for x in range(8)], 1)
        )
        ft = jnp.concatenate([pre[80 * x + 64 : 80 * x + 80] for x in range(8)], 1)
        h1h, h1l = split(h1)
        h2 = jnp.tanh(
            jnp.dot(
                w2s[...], jnp.concatenate([h1h, h1h, h1l], 0), preferred_element_type=F32
            )
        )
        w3 = w3_ref[...]
        o = jnp.zeros((8, 128), F32)
        for x in range(8):
            row = jnp.sum(h2[:, 128 * x : 128 * x + 128] * w3, 0, keepdims=True)
            o = jnp.where(sub == x, row, o)
        decay = jnp.exp(-jnp.abs(o))
        eddy = 0.5 * (jnp.maximum(o, 0.0) + jnp.log1p(decay))
        sig = jnp.where(o >= 0.0, 1.0, decay) / (1.0 + decay)

        rho = rho_ref[g]
        prs = prs_ref[g]
        u = [vel_ref[i, g] for i in range(3)]
        ct = [ct_ref[i, g] for i in range(5)]
        q = u[0] * u[0] + u[1] * u[1] + u[2] * u[2]
        energy = prs / 0.4 + 0.5 * rho * q
        stag = energy + prs
        att = rho * eddy
        s = [[TIME_STEP * der[k, 4 + m, g] for m in range(5)] for k in range(3)]
        grad3 = [der[k, 3, g] for k in range(3)]
        flux_refs = (fx, fy, fz)
        att_bar = jnp.zeros((8, 128), F32)
        rho_bar = jnp.zeros((8, 128), F32)
        stag_bar = s[0][4] * u[0] + s[1][4] * u[1] + s[2][4] * u[2]
        for k in range(3):
            ref = flux_refs[k]
            mass = rho * u[k]
            ref[4, g] = mass
            inner = s[k][0]
            for i in range(3):
                value = mass * u[i] - att * feats[3 * k + i]
                if i == k:
                    value = value + prs
                ref[5 + i, g] = value
                att_bar = att_bar - s[k][1 + i] * feats[3 * k + i]
                inner = inner + s[k][1 + i] * u[i]
            ref[8, g] = stag * u[k] - 3.5 * att * grad3[k]
            ref[3, g] = -3.5 * att * s[k][4]
            att_bar = att_bar - 3.5 * s[k][4] * grad3[k]
            rho_bar = rho_bar + inner * u[k]
        for j in range(3):
            t = s[j][0] + ct[1 + j] + (stag_bar + ct[4]) * u[j]
            for i in range(3):
                t = t + (s[j][1 + i] + s[i][1 + j]) * u[i]
            avel_ref[j, g] = rho * t + stag * s[j][4]
        aprs_ref[g] = s[0][1] + s[1][2] + s[2][3] + stag_bar + (stag_bar + ct[4]) / 0.4
        arho_ref[g] = (
            rho_bar + 0.5 * q * (stag_bar + ct[4]) + att_bar * eddy + ct[0]
            + ct[1] * u[0] + ct[2] * u[1] + ct[3] * u[2]
        )
        next_ref[0, g] = rho
        for i in range(3):
            next_ref[1 + i, g] = rho * u[i]
        next_ref[4, g] = energy

        ob = 0.5 * att_bar * rho * sig
        seeds = []
        outer = w3acc[...]
        for x in range(8):
            row = jnp.broadcast_to(ob[x : x + 1], (HID, 128))
            seeds.append(row * w3)
            outer = outer + row * h2[:, 128 * x : 128 * x + 128]
        w3acc[...] = outer
        a2 = jnp.concatenate(seeds, 1) * (1.0 - h2 * h2)
        a2h, a2l = split(a2)
        a1 = jnp.dot(
            w2ts[...], jnp.concatenate([a2h, a2h, a2l], 0), preferred_element_type=F32
        ) * (1.0 - h1 * h1)
        a1h, a1l = split(a1)
        tall_h = jnp.concatenate([a1h[:, 128 * x : 128 * x + 128] for x in range(8)], 0)
        tall_l = jnp.concatenate([a1l[:, 128 * x : 128 * x + 128] for x in range(8)], 0)
        fbar = jnp.dot(
            b1s[...], jnp.concatenate([tall_h, tall_h, tall_l], 0), preferred_element_type=F32
        )
        for k in range(3):
            for i in range(3):
                c = 3 * k + i
                flux_refs[k][i, g] = fbar[8 * c : 8 * c + 8] - att * s[k][1 + i]
        fth, ftl = split(ft)
        acc[:, :160] = acc[:, :160] + lax.dot_general(
            jnp.concatenate([a2h, a2l, a1h, a1l], 0),
            jnp.concatenate([h1h, h1l, fth, ftl], 0),
            (((1,), (1,)), ((), ())),
            preferred_element_type=F32,
        )
        return carry

    lax.fori_loop(0, 16, group, 0, unroll=2)

    wlane = lax.broadcasted_iota(jnp.int32, (HID, 128), 1)
    mid_w = acc[0:64, 0:128] + acc[64:128, 0:128] + pltpu.roll(acc[0:64, 0:128], 64, 1)
    in_w = acc[128:192, 128:256] + acc[192:256, 128:256]
    in_w = in_w + pltpu.roll(acc[128:192, 128:256], 112, 1)
    in_w = pltpu.roll(in_w, 64, 1)
    out_w = jnp.sum(w3acc[...], 1, keepdims=True)
    mine = jnp.where(
        wlane < 64, mid_w, jnp.where(wlane < 80, in_w, jnp.where(wlane == 80, out_w, 0.0))
    )

    def exchange(buf, axis, value):
        buf[me[axis]] = value
        return [
            remote(buf.at[me[axis]], buf.at[me[axis]], axis, offset)
            for offset in range(1, sizes[axis])
        ]

    def total_of(buf, axis):
        value = buf[0]
        for i in range(1, sizes[axis]):
            value = value + buf[i]
        return value

    def put1(j, value):
        back[j] = value

    solve_x(1, fx, put1)
    cx = start_x(1)
    cz = send_z(1, fz)
    ez = exchange(part_z, "gz", mine)
    pack_y(1, fy)
    cy = start_y(1)
    for c in ez:
        c.wait_recv()
    ex = exchange(part_x, "gx", total_of(part_z, "gz"))
    for c in cz:
        c.wait_recv()
    for j in range(FIELDS):
        back[j] = back[j] + dz(1, fz, j)
    for c in cy:
        c.wait_recv()
    for j in range(FIELDS):
        back[j] = back[j] + dy(1, fy, j)
    for c in ex:
        c.wait_recv()
    ey = exchange(part_y, "gy", total_of(part_x, "gx"))
    for c in cx:
        c.wait_recv()

    def add1(j, value):
        back[j] = back[j] + value

    add_x(1, add1)
    for m in range(5):
        next_ref[m] = next_ref[m] - TIME_STEP * back[4 + m]
    for j in range(3):
        avel_ref[j] = avel_ref[j] - back[j]
    inv = 1.0 / rho_ref[...]
    heat = back[3] * inv
    aprs_ref[...] = aprs_ref[...] - heat
    arho_ref[...] = arho_ref[...] + heat * f0[3]
    for c in ey:
        c.wait_recv()
    cells = 16384 * gxn * gyn * gzn
    wg_ref[...] = total_of(part_y, "gy") * (1.0 / math.sqrt(cells))
    pending += ez + cz + cy + cx + ex + ey
    for c in pending:
        c.wait_send()


def local(dims, rho, vel, prs, ct, w_in, w_mid, w_out):
    gxn, gyn, gzn = dims
    zc, xc, yc = rho.shape
    reach = 40 // xc + 2
    if 2 * reach + 1 >= gxn:
        offsets = list(range(1, gxn - 1)) + [-1]
    else:
        offsets = list(range(1, reach + 1)) + list(range(-reach, 0))
    offsets = tuple(offsets)
    n_off = len(offsets)
    xfull, xadd = x_tables(xc, zc, gxn)
    feat = jnp.concatenate(
        [jnp.pad(w_in, ((0, 0), (0, 1))), jnp.asarray(np.eye(16, 10), F32)], 0
    )
    eye = jnp.asarray(np.eye(8), F32)
    w1 = (eye[:, None, None, :] * feat[None, :, :, None]).reshape(640, 80)
    w1 = jnp.concatenate([w1, w1, w1], 1)
    b1 = jnp.pad(w_in, ((0, 0), (0, 1))).T[:, None, None, :] * eye[None, :, :, None]
    b1 = b1.reshape(80, 512)
    b1 = jnp.concatenate([b1, b1, b1], 1)
    w2 = jnp.concatenate([w_mid, w_mid, w_mid], 1)
    w2t = jnp.concatenate([w_mid.T, w_mid.T, w_mid.T], 1)
    w3 = jnp.broadcast_to(w_out[:, None], (HID, 128))
    block = (16, 8, 128)
    n_sem = 2 * (n_off + 4) + (gxn - 1) + (gyn - 1) + (gzn - 1)
    vmem = pl.BlockSpec(memory_space=pltpu.VMEM)
    out = pl.pallas_call(
        functools.partial(kernel, dims, offsets),
        out_shape=(
            jax.ShapeDtypeStruct((5,) + block, F32),
            jax.ShapeDtypeStruct(block, F32),
            jax.ShapeDtypeStruct((3,) + block, F32),
            jax.ShapeDtypeStruct(block, F32),
            jax.ShapeDtypeStruct((HID, 128), F32),
        ),
        in_specs=[vmem] * 11,
        out_specs=(vmem,) * 5,
        scratch_shapes=[
            pltpu.VMEM((FIELDS,) + block, F32),
            pltpu.VMEM((FIELDS,) + block, F32),
            pltpu.VMEM((FIELDS,) + block, F32),
            pltpu.VMEM((FIELDS,) + block, F32),
            pltpu.VMEM((3, FIELDS) + block, F32),
            pltpu.VMEM((FIELDS,) + block, F32),
            pltpu.VMEM((640, 240), BF16),
            pltpu.VMEM((HID, 192), BF16),
            pltpu.VMEM((HID, 192), BF16),
            pltpu.VMEM((80, 1536), BF16),
            pltpu.VMEM((256, 256), F32),
            pltpu.VMEM((HID, 128), F32),
            pltpu.VMEM((2, 4, FIELDS, 8, 128), F32),
            pltpu.VMEM((2, n_off, 4, FIELDS, 8, 128), F32),
            pltpu.VMEM((2, 4, 8, 128), F32),
            pltpu.VMEM((2, 4, 8, 128), F32),
            pltpu.VMEM((2, 4, 8, 128), F32),
            pltpu.VMEM((2, 4, 8, 128), F32),
            pltpu.VMEM((2, FIELDS, 6, 8, 128), F32),
            pltpu.VMEM((2, FIELDS, 6, 8, 128), F32),
            pltpu.VMEM((gzn, HID, 128), F32),
            pltpu.VMEM((gxn, HID, 128), F32),
            pltpu.VMEM((gyn, HID, 128), F32),
            pltpu.SemaphoreType.DMA((n_sem,)),
            pltpu.SemaphoreType.DMA((n_sem,)),
        ],
        compiler_params=pltpu.CompilerParams(
            collective_id=0, has_side_effects=True, vmem_limit_bytes=40 * 1024 * 1024
        ),
    )(
        rho.reshape(block), vel.reshape((3,) + block), prs.reshape(block), ct.reshape((5,) + block),
        jnp.asarray(xfull), jnp.asarray(xadd), w1, w2, w2t, b1, w3,
    )
    nxt, arho, avel, aprs, wg = out
    return (
        nxt.reshape(ct.shape),
        arho.reshape(rho.shape),
        avel.reshape(vel.shape),
        aprs.reshape(prs.shape),
        wg[:, 64:73],
        wg[:, :64],
        wg[:, 80],
    )


def solution(mesh):
    dims = tuple(mesh.shape[axis] for axis in ("gx", "gy", "gz"))
    placed = (
        P("gz", "gx", "gy"),
        P(None, "gz", "gx", "gy"),
        P("gz", "gx", "gy"),
        P(None, "gz", "gx", "gy"),
        P(),
        P(),
        P(),
    )
    return jax.shard_map(
        functools.partial(local, dims),
        mesh=mesh,
        in_specs=placed,
        out_specs=(
            P(None, "gz", "gx", "gy"),
            P("gz", "gx", "gy"),
            P(None, "gz", "gx", "gy"),
            P("gz", "gx", "gy"),
            P(),
            P(),
            P(),
        ),
        check_vma=False,
    )
```

```python
import functools
import math

import jax
import jax.numpy as jnp
import ml_dtypes
import numpy as np
from jax import lax
from jax.experimental import pallas as pl
from jax.experimental.pallas import tpu as pltpu
from jax.sharding import PartitionSpec as P

TIME_STEP = 0.1
ALPHA = 1.0 / 3.0
MESH = pl.DeviceIdType.MESH
F32 = jnp.float32
BF16 = jnp.bfloat16
ROOT = (-1.0 + math.sqrt(1.0 - 4.0 * ALPHA**2)) / (2.0 * ALPHA)
FIELDS = 9
HID = 64


def split_np(a):
    hi = a.astype(ml_dtypes.bfloat16)
    lo = (a - hi.astype(np.float64)).astype(ml_dtypes.bfloat16)
    return np.concatenate([hi, lo, hi], 1)


def split(x):
    hi = x.astype(BF16)
    lo = (x - hi.astype(F32)).astype(BF16)
    return hi, lo


def stack3(x):
    hi, lo = split(x)
    return jnp.concatenate([hi, hi, lo], 0)


def x_tables(xc, zc, groups):
    n = xc * groups
    r = ROOT
    c0 = 1.0 + 2.0 * ALPHA * r
    period = 1.0 - r**n
    gain = (7.0 / 9.0 * (r - 1 / r) + 1.0 / 36.0 * (r**2 - r**-2)) / c0
    fix = (1 / r - r) / 36.0 / c0
    i = np.arange(xc)
    d = i[:, None] - i[None, :]
    own = np.where(d == 0, 0.0, np.sign(d) * gain * r ** np.abs(d))
    own = own + np.where(np.abs(d) == 1, np.sign(d) * fix, 0.0)
    own = own + gain * (r ** (d + n) - r ** (n - d)) / period
    eye = np.eye(zc)
    last = np.zeros((1, xc))
    last[0, -1] = 1.0
    first = np.zeros((1, xc))
    first[0, 0] = 1.0
    right = (r ** (xc - 1 - i))[None]
    left = (r**i)[None]
    full = np.concatenate(
        [np.kron(eye, own)] + [np.kron(eye, row) for row in (last, right, left, first)], 0
    )
    add_last = np.zeros((xc, 1))
    add_last[0] = fix
    add_first = np.zeros((xc, 1))
    add_first[-1] = -fix
    add = np.concatenate(
        [
            np.kron(eye, column)
            for column in (
                add_last,
                (gain * r ** (i + 1))[:, None],
                (-gain * r ** (xc - i))[:, None],
                add_first,
            )
        ],
        1,
    )
    return split_np(full), split_np(add)


def kernel(
    dims, offsets, rho_ref, vel_ref, prs_ref, ct_ref, xfull_ref, xadd_ref, w1_ref, w2_ref, w2t_ref,
    b1_ref, w3_ref, next_ref, arho_ref, avel_ref, aprs_ref, wg_ref,
    f0, fx, fy, fz, der, back, w1s, w2s, w2ts, b1s, acc, w3acc,
    mom, momr, ypl, ypr, yl, yr, zlo, zhi, part_z, part_x, part_y, send_sem, recv_sem,
):
    gxn, gyn, gzn = dims
    sizes = {"gx": gxn, "gy": gyn, "gz": gzn}
    me = {axis: lax.axis_index(axis) for axis in sizes}
    lane = lax.broadcasted_iota(jnp.int32, (1, 1, 128), 2)

    def other(axis, offset):
        return {axis: lax.rem(me[axis] + (offset + sizes[axis]), sizes[axis])}

    barrier = pltpu.get_barrier_semaphore()
    total = 0
    for axis in sizes:
        for offset in range(1, sizes[axis]):
            pl.semaphore_signal(barrier, inc=1, device_id=other(axis, offset), device_id_type=MESH)
            total += 1

    used = [0]

    def remote(src, dst, axis, offset):
        k = used[0]
        used[0] += 1
        copy = pltpu.make_async_remote_copy(
            src_ref=src, dst_ref=dst, send_sem=send_sem.at[k], recv_sem=recv_sem.at[k],
            device_id=other(axis, offset), device_id_type=MESH,
        )
        copy.start()
        return copy

    pending = []

    def send_z(ph, src):
        a = remote(src.at[:, 10:16], zlo.at[ph], "gz", 1)
        b = remote(src.at[:, 0:6], zhi.at[ph], "gz", -1)
        return [a, b]

    def pack_y(ph, src):
        for j in range(FIELDS):
            for q in range(4):
                block = src[j, 4 * q : 4 * q + 4]
                at = 32 * q + 3 * j
                inside = (lane >= at) & (lane < at + 3)
                hi_edge = pltpu.roll(block, (at - 125) % 128, 2)
                lo_edge = pltpu.roll(block, at, 2) if at else block
                if j == 0 and q == 0:
                    vl, vr = hi_edge, lo_edge
                    keep = [vl, vr]
                else:
                    keep = [
                        jnp.where(inside, hi_edge, keep[0]),
                        jnp.where(inside, lo_edge, keep[1]),
                    ]
        ypl[ph] = keep[0]
        ypr[ph] = keep[1]

    def start_y(ph):
        return [
            remote(ypl.at[ph], yl.at[ph], "gy", 1),
            remote(ypr.at[ph], yr.at[ph], "gy", -1),
        ]

    def solve_x(ph, src, put):
        def one(j, carry):
            y = jnp.dot(
                xfull_ref[...], stack3(src[j].reshape(128, 128)), preferred_element_type=F32
            )
            put(j, y[:128].reshape(16, 8, 128))
            for m in range(4):
                mom[ph, m, j] = y[128 + 8 * m : 136 + 8 * m]
            return carry

        lax.fori_loop(0, FIELDS, one, 0, unroll=9)

    def start_x(ph):
        copies = []
        for slot, offset in enumerate(offsets):
            lo = 0 if offset == 1 else 1
            hi = 4 if offset == -1 else 3
            copies.append(
                remote(mom.at[ph, lo:hi], momr.at[ph, slot, lo:hi], "gx", offset)
            )
        return copies

    def dy(ph, src, j):
        outs = []
        for q in range(4):
            at = 32 * q + 3 * j
            f = src[j, 4 * q : 4 * q + 4]
            el = pltpu.roll(yl[ph], (125 - at) % 128, 2)
            er = pltpu.roll(yr[ph], (-at) % 128, 2) if at else yr[ph]

            def ahead(s):
                return pltpu.roll(jnp.where(lane < s, er, f), 128 - s, 2)

            def behind(s):
                return pltpu.roll(jnp.where(lane >= 128 - s, el, f), s, 2)

            outs.append(
                0.75 * (ahead(1) - behind(1))
                - 0.15 * (ahead(2) - behind(2))
                + (1.0 / 60.0) * (ahead(3) - behind(3))
            )
        return jnp.concatenate(outs, 0)

    def dz(ph, src, j):
        ext = jnp.concatenate([zlo[ph, j], src[j], zhi[ph, j]], 0)

        def shifted(s):
            return ext[6 + 2 * s : 22 + 2 * s]

        return (
            0.75 * (shifted(1) - shifted(-1))
            - 0.15 * (shifted(2) - shifted(-2))
            + (1.0 / 60.0) * (shifted(3) - shifted(-3))
        )

    period = 1.0 - ROOT ** (16 * gxn)

    def add_x(ph, add):
        def one(j, carry):
            va = jnp.zeros((8, 128), F32)
            vb = jnp.zeros((8, 128), F32)
            for slot, offset in enumerate(offsets):
                wa = ROOT ** (16 * (offset % gxn - 1)) / period
                wb = ROOT ** (16 * ((-offset) % gxn - 1)) / period
                va = va + wa * momr[ph, slot, 1, j]
                vb = vb + wb * momr[ph, slot, 2, j]
            rows = jnp.concatenate(
                [
                    momr[ph, offsets.index(1), 0, j],
                    va,
                    vb,
                    momr[ph, offsets.index(-1), 3, j],
                ],
                0,
            )
            y = jnp.dot(xadd_ref[...], stack3(rows), preferred_element_type=F32)
            add(j, y.reshape(16, 8, 128))
            return carry

        lax.fori_loop(0, FIELDS, one, 0, unroll=9)

    f0[0:3] = vel_ref[...]
    f0[3] = prs_ref[...] / rho_ref[...]
    f0[4:9] = ct_ref[...]

    def put0(j, value):
        der[0, j] = value

    solve_x(0, f0, put0)
    pack_y(0, f0)
    pl.semaphore_wait(barrier, total)
    cx = start_x(0)
    cz = send_z(0, f0)
    cy = start_y(0)
    pending += cz + cy + cx

    def halves(src, dst, third):
        x = src[...]
        hi, lo = split(x)
        col = lax.broadcasted_iota(jnp.int32, x.shape, 1)
        mid = (col >= third) & (col < 2 * third)
        dst[...] = jnp.where(mid, lo.astype(F32), hi.astype(F32)).astype(BF16)

    halves(w1_ref, w1s, 80)
    halves(w2_ref, w2s, HID)
    halves(w2t_ref, w2ts, HID)
    b1_hi, b1_lo = split(b1_ref[...])
    b1s[:, 0:512] = b1_hi
    b1s[:, 512:1024] = b1_lo
    b1s[:, 1024:1536] = b1_hi
    acc[...] = jnp.zeros_like(acc)
    w3acc[...] = jnp.zeros_like(w3acc)

    for c in cz:
        c.wait_recv()
    for j in range(FIELDS):
        der[2, j] = dz(0, f0, j)
    for c in cy:
        c.wait_recv()
    for j in range(FIELDS):
        der[1, j] = dy(0, f0, j)
    for c in cx:
        c.wait_recv()

    def add0(j, value):
        der[0, j] = der[0, j] + value

    add_x(0, add0)

    sub = lax.broadcasted_iota(jnp.int32, (8, 128), 0)

    def group(g, carry):
        feats = [der[k, i, g] for k in range(3) for i in range(3)]
        pre = jnp.dot(
            w1s[...],
            stack3(jnp.concatenate(feats + [jnp.zeros((8, 128), F32)], 0)),
            preferred_element_type=F32,
        )
        h1 = jnp.tanh(
            jnp.concatenate([pre[80 * x : 80 * x + 64] for x in range(8)], 1)
        )
        ft = jnp.concatenate([pre[80 * x + 64 : 80 * x + 80] for x in range(8)], 1)
        h1h, h1l = split(h1)
        h2 = jnp.tanh(
            jnp.dot(
                w2s[...], jnp.concatenate([h1h, h1h, h1l], 0), preferred_element_type=F32
            )
        )
        w3 = w3_ref[...]
        o = jnp.zeros((8, 128), F32)
        for x in range(8):
            row = jnp.sum(h2[:, 128 * x : 128 * x + 128] * w3, 0, keepdims=True)
            o = jnp.where(sub == x, row, o)
        decay = jnp.exp(-jnp.abs(o))
        eddy = 0.5 * (jnp.maximum(o, 0.0) + jnp.log1p(decay))
        sig = jnp.where(o >= 0.0, 1.0, decay) / (1.0 + decay)

        rho = rho_ref[g]
        prs = prs_ref[g]
        u = [vel_ref[i, g] for i in range(3)]
        ct = [ct_ref[i, g] for i in range(5)]
        q = u[0] * u[0] + u[1] * u[1] + u[2] * u[2]
        energy = prs / 0.4 + 0.5 * rho * q
        stag = energy + prs
        att = rho * eddy
        s = [[TIME_STEP * der[k, 4 + m, g] for m in range(5)] for k in range(3)]
        grad3 = [der[k, 3, g] for k in range(3)]
        flux_refs = (fx, fy, fz)
        att_bar = jnp.zeros((8, 128), F32)
        rho_bar = jnp.zeros((8, 128), F32)
        stag_bar = s[0][4] * u[0] + s[1][4] * u[1] + s[2][4] * u[2]
        for k in range(3):
            ref = flux_refs[k]
            mass = rho * u[k]
            ref[4, g] = mass
            inner = s[k][0]
            for i in range(3):
                value = mass * u[i] - att * feats[3 * k + i]
                if i == k:
                    value = value + prs
                ref[5 + i, g] = value
                att_bar = att_bar - s[k][1 + i] * feats[3 * k + i]
                inner = inner + s[k][1 + i] * u[i]
            ref[8, g] = stag * u[k] - 3.5 * att * grad3[k]
            ref[3, g] = -3.5 * att * s[k][4]
            att_bar = att_bar - 3.5 * s[k][4] * grad3[k]
            rho_bar = rho_bar + inner * u[k]
        for j in range(3):
            t = s[j][0] + ct[1 + j] + (stag_bar + ct[4]) * u[j]
            for i in range(3):
                t = t + (s[j][1 + i] + s[i][1 + j]) * u[i]
            avel_ref[j, g] = rho * t + stag * s[j][4]
        aprs_ref[g] = s[0][1] + s[1][2] + s[2][3] + stag_bar + (stag_bar + ct[4]) / 0.4
        arho_ref[g] = (
            rho_bar + 0.5 * q * (stag_bar + ct[4]) + att_bar * eddy + ct[0]
            + ct[1] * u[0] + ct[2] * u[1] + ct[3] * u[2]
        )
        next_ref[0, g] = rho
        for i in range(3):
            next_ref[1 + i, g] = rho * u[i]
        next_ref[4, g] = energy

        ob = 0.5 * att_bar * rho * sig
        seeds = []
        outer = w3acc[...]
        for x in range(8):
            row = jnp.broadcast_to(ob[x : x + 1], (HID, 128))
            seeds.append(row * w3)
            outer = outer + row * h2[:, 128 * x : 128 * x + 128]
        w3acc[...] = outer
        a2 = jnp.concatenate(seeds, 1) * (1.0 - h2 * h2)
        a2h, a2l = split(a2)
        a1 = jnp.dot(
            w2ts[...], jnp.concatenate([a2h, a2h, a2l], 0), preferred_element_type=F32
        ) * (1.0 - h1 * h1)
        a1h, a1l = split(a1)
        tall_h = jnp.concatenate([a1h[:, 128 * x : 128 * x + 128] for x in range(8)], 0)
        tall_l = jnp.concatenate([a1l[:, 128 * x : 128 * x + 128] for x in range(8)], 0)
        fbar = jnp.dot(
            b1s[...], jnp.concatenate([tall_h, tall_h, tall_l], 0), preferred_element_type=F32
        )
        for k in range(3):
            for i in range(3):
                c = 3 * k + i
                flux_refs[k][i, g] = fbar[8 * c : 8 * c + 8] - att * s[k][1 + i]
        fth, ftl = split(ft)
        acc[:, :160] = acc[:, :160] + lax.dot_general(
            jnp.concatenate([a2h, a2l, a1h, a1l], 0),
            jnp.concatenate([h1h, h1l, fth, ftl], 0),
            (((1,), (1,)), ((), ())),
            preferred_element_type=F32,
        )
        return carry

    lax.fori_loop(0, 16, group, 0, unroll=4)

    wlane = lax.broadcasted_iota(jnp.int32, (HID, 128), 1)
    mid_w = acc[0:64, 0:128] + acc[64:128, 0:128] + pltpu.roll(acc[0:64, 0:128], 64, 1)
    in_w = acc[128:192, 128:256] + acc[192:256, 128:256]
    in_w = in_w + pltpu.roll(acc[128:192, 128:256], 112, 1)
    in_w = pltpu.roll(in_w, 64, 1)
    out_w = jnp.sum(w3acc[...], 1, keepdims=True)
    mine = jnp.where(
        wlane < 64, mid_w, jnp.where(wlane < 80, in_w, jnp.where(wlane == 80, out_w, 0.0))
    )

    def exchange(buf, axis, value):
        buf[me[axis]] = value
        return [
            remote(buf.at[me[axis]], buf.at[me[axis]], axis, offset)
            for offset in range(1, sizes[axis])
        ]

    def total_of(buf, axis):
        value = buf[0]
        for i in range(1, sizes[axis]):
            value = value + buf[i]
        return value

    def put1(j, value):
        back[j] = value

    solve_x(1, fx, put1)
    cx = start_x(1)
    cz = send_z(1, fz)
    ez = exchange(part_z, "gz", mine)
    pack_y(1, fy)
    cy = start_y(1)
    for c in ez:
        c.wait_recv()
    ex = exchange(part_x, "gx", total_of(part_z, "gz"))
    for c in cz:
        c.wait_recv()
    for j in range(FIELDS):
        back[j] = back[j] + dz(1, fz, j)
    for c in cy:
        c.wait_recv()
    for j in range(FIELDS):
        back[j] = back[j] + dy(1, fy, j)
    for c in ex:
        c.wait_recv()
    ey = exchange(part_y, "gy", total_of(part_x, "gx"))
    for c in cx:
        c.wait_recv()

    def add1(j, value):
        back[j] = back[j] + value

    add_x(1, add1)
    for m in range(5):
        next_ref[m] = next_ref[m] - TIME_STEP * back[4 + m]
    for j in range(3):
        avel_ref[j] = avel_ref[j] - back[j]
    inv = 1.0 / rho_ref[...]
    heat = back[3] * inv
    aprs_ref[...] = aprs_ref[...] - heat
    arho_ref[...] = arho_ref[...] + heat * f0[3]
    for c in ey:
        c.wait_recv()
    cells = 16384 * gxn * gyn * gzn
    wg_ref[...] = total_of(part_y, "gy") * (1.0 / math.sqrt(cells))
    pending += ez + cz + cy + cx + ex + ey
    for c in pending:
        c.wait_send()


def local(dims, rho, vel, prs, ct, w_in, w_mid, w_out):
    gxn, gyn, gzn = dims
    zc, xc, yc = rho.shape
    reach = 40 // xc + 2
    if 2 * reach + 1 >= gxn:
        offsets = list(range(1, gxn - 1)) + [-1]
    else:
        offsets = list(range(1, reach + 1)) + list(range(-reach, 0))
    offsets = tuple(offsets)
    n_off = len(offsets)
    xfull, xadd = x_tables(xc, zc, gxn)
    feat = jnp.concatenate(
        [jnp.pad(w_in, ((0, 0), (0, 1))), jnp.asarray(np.eye(16, 10), F32)], 0
    )
    eye = jnp.asarray(np.eye(8), F32)
    w1 = (eye[:, None, None, :] * feat[None, :, :, None]).reshape(640, 80)
    w1 = jnp.concatenate([w1, w1, w1], 1)
    b1 = jnp.pad(w_in, ((0, 0), (0, 1))).T[:, None, None, :] * eye[None, :, :, None]
    b1 = b1.reshape(80, 512)
    w2 = jnp.concatenate([w_mid, w_mid, w_mid], 1)
    w2t = jnp.concatenate([w_mid.T, w_mid.T, w_mid.T], 1)
    w3 = jnp.broadcast_to(w_out[:, None], (HID, 128))
    block = (16, 8, 128)
    n_sem = 2 * (n_off + 4) + (gxn - 1) + (gyn - 1) + (gzn - 1)
    vmem = pl.BlockSpec(memory_space=pltpu.VMEM)
    out = pl.pallas_call(
        functools.partial(kernel, dims, offsets),
        out_shape=(
            jax.ShapeDtypeStruct((5,) + block, F32),
            jax.ShapeDtypeStruct(block, F32),
            jax.ShapeDtypeStruct((3,) + block, F32),
            jax.ShapeDtypeStruct(block, F32),
            jax.ShapeDtypeStruct((HID, 128), F32),
        ),
        in_specs=[vmem] * 11,
        out_specs=(vmem,) * 5,
        scratch_shapes=[
            pltpu.VMEM((FIELDS,) + block, F32),
            pltpu.VMEM((FIELDS,) + block, F32),
            pltpu.VMEM((FIELDS,) + block, F32),
            pltpu.VMEM((FIELDS,) + block, F32),
            pltpu.VMEM((3, FIELDS) + block, F32),
            pltpu.VMEM((FIELDS,) + block, F32),
            pltpu.VMEM((640, 240), BF16),
            pltpu.VMEM((HID, 192), BF16),
            pltpu.VMEM((HID, 192), BF16),
            pltpu.VMEM((80, 1536), BF16),
            pltpu.VMEM((256, 256), F32),
            pltpu.VMEM((HID, 128), F32),
            pltpu.VMEM((2, 4, FIELDS, 8, 128), F32),
            pltpu.VMEM((2, n_off, 4, FIELDS, 8, 128), F32),
            pltpu.VMEM((2, 4, 8, 128), F32),
            pltpu.VMEM((2, 4, 8, 128), F32),
            pltpu.VMEM((2, 4, 8, 128), F32),
            pltpu.VMEM((2, 4, 8, 128), F32),
            pltpu.VMEM((2, FIELDS, 6, 8, 128), F32),
            pltpu.VMEM((2, FIELDS, 6, 8, 128), F32),
            pltpu.VMEM((gzn, HID, 128), F32),
            pltpu.VMEM((gxn, HID, 128), F32),
            pltpu.VMEM((gyn, HID, 128), F32),
            pltpu.SemaphoreType.DMA((n_sem,)),
            pltpu.SemaphoreType.DMA((n_sem,)),
        ],
        compiler_params=pltpu.CompilerParams(
            collective_id=0, has_side_effects=True, vmem_limit_bytes=40 * 1024 * 1024
        ),
    )(
        rho.reshape(block), vel.reshape((3,) + block), prs.reshape(block), ct.reshape((5,) + block),
        jnp.asarray(xfull), jnp.asarray(xadd), w1, w2, w2t, b1, w3,
    )
    nxt, arho, avel, aprs, wg = out
    return (
        nxt.reshape(ct.shape),
        arho.reshape(rho.shape),
        avel.reshape(vel.shape),
        aprs.reshape(prs.shape),
        wg[:, 64:73],
        wg[:, :64],
        wg[:, 80],
    )


def solution(mesh):
    dims = tuple(mesh.shape[axis] for axis in ("gx", "gy", "gz"))
    placed = (
        P("gz", "gx", "gy"),
        P(None, "gz", "gx", "gy"),
        P("gz", "gx", "gy"),
        P(None, "gz", "gx", "gy"),
        P(),
        P(),
        P(),
    )
    return jax.shard_map(
        functools.partial(local, dims),
        mesh=mesh,
        in_specs=placed,
        out_specs=(
            P(None, "gz", "gx", "gy"),
            P("gz", "gx", "gy"),
            P(None, "gz", "gx", "gy"),
            P("gz", "gx", "gy"),
            P(),
            P(),
            P(),
        ),
        check_vma=False,
    )
```
